128 devices in a mesh: dp: 4 (over z), ctx: 8 (over y, core), tensor: 4 (over x).
Axes of the slice: x: 4, y: 4, z: 4, core: 2. Of those that a mesh axis runs over, the one named last changes fastest.
Arguments:
- queries: bfloat16 [16384, 64, 128], P(('dp', 'ctx', 'tensor')), parts along dimension 0, may hold values from -8 to 8
- key_states: bfloat16 [16384, 8, 128], P(('dp', 'ctx', 'tensor')), parts along dimension 0, may hold values from -8 to 8
- value_states: bfloat16 [16384, 8, 128], P(('dp', 'ctx', 'tensor')), parts along dimension 0, may hold values from -6 to 6
- grad_out: bfloat16 [16384, 64, 128], P(('dp', 'ctx', 'tensor')), parts along dimension 0, may hold values from -6 to 6
- doc_lengths: int32 [36], P('dp'), parts along dimension 0, may hold values from 4 to 1024, as said below
Outputs:
- attended: bfloat16 [16384, 64, 128], P(('dp', 'ctx', 'tensor')), parts along dimension 0
- grad_queries: bfloat16 [16384, 64, 128], P(('dp', 'ctx', 'tensor')), parts along dimension 0
- grad_keys: bfloat16 [16384, 8, 128], P(('dp', 'ctx', 'tensor')), parts along dimension 0
- grad_values: bfloat16 [16384, 8, 128], P(('dp', 'ctx', 'tensor')), parts along dimension 0
The draws below stay inside these ranges and needn't reach their ends.
There are 4 independent parts, one for each index of `dp`. The reference program is written for one: setup_inputs(seed, part) draws one part's arguments, and reference() takes and returns one part's arrays. A program takes and returns all parts, laid end to end along the dimension named above; each array names one. Nothing has to cross between parts.
Inputs may be any that keep to these rules, and one draw needn't show every extreme that they name: `doc_lengths`: 9 lengths adding up to 4096; one document has exactly 1024 tokens; the others form pairs whose lengths add up to 768.
All inputs are finite; a program needn't handle non-finite values.
Results may differ from the reference program's by a relative error of at most 0.039.
Values may be sent and summed in bfloat16 or wider, within the bound.
No kernel may reach another device: no remote copies, remote signals or barrier semaphores. Data moves between devices by JAX's collectives and lax.ppermute only.
A program may use at most 192 MiB of HBM per device.

```python
import math
import jax
import jax.numpy as jnp
from jax import lax

H = 64
KVH = 8
HD = 128
TOKENS = 4096
DOCS = 9


def document_lengths(key):
    key = jax.random.fold_in(key, 101)
    pair_total = 3 * TOKENS // 16
    pair_count = (DOCS - 1) // 2
    first = jax.random.randint(jax.random.fold_in(key, 1), (pair_count,), pair_total // 4, 3 * pair_total // 4 + 1).astype(jnp.int32)
    first = first.at[0].set(4)
    lengths = jnp.concatenate([jnp.full((1,), TOKENS // 4, jnp.int32), first, (pair_total - first).astype(jnp.int32)])
    order = jax.random.permutation(jax.random.fold_in(key, 2), DOCS)
    return lengths[order]


def draw_doc_lengths(key, part):
    return document_lengths(key)


def draw_queries(key, part):
    key = jax.random.fold_in(key, 3)
    base = jnp.clip(jax.random.normal(key, (TOKENS, H, HD), jnp.float32), -5.0, 5.0)
    return base.astype(jnp.bfloat16)


def draw_key_states(key, part):
    key = jax.random.fold_in(key, 4)
    base = jnp.clip(jax.random.normal(key, (TOKENS, KVH, HD), jnp.float32), -5.0, 5.0)
    return base.astype(jnp.bfloat16)


def block_levels(key, shape, pieces, least, top_value):
    def one(position, parts):
        draws = jax.random.uniform(jax.random.fold_in(jax.random.fold_in(key, 6), position), (parts,), jnp.float32, least / len(pieces), top_value / len(pieces))
        return jnp.repeat(jnp.exp(draws), shape[position] // parts).reshape((-1,) + (1,) * (len(shape) - position - 1))

    gain = one(*pieces[0])
    for cut in pieces[1:]:
        gain = gain * one(*cut)
    return gain


def normal_values(rng, shape, width, most, pieces=(), held_as=jnp.bfloat16):
    values = width * jax.random.normal(rng, shape, jnp.float32)
    if pieces:
        values = values * block_levels(rng, shape, pieces, -0.22, 0.18)
    return jnp.clip(values, -most, most).astype(held_as)


def setup_inputs(seed: int = 0, part: int = 0) -> dict:
    keys = jax.random.split(jax.random.key(seed), 6)
    own_keys = jax.random.split(jax.random.fold_in(keys[5], part), 6)
    return {
        "queries": draw_queries(jax.random.fold_in(jax.random.fold_in(keys[5], part), 71), part),
        "key_states": draw_key_states(jax.random.fold_in(jax.random.fold_in(keys[5], part), 71), part),
        "value_states": normal_values(own_keys[2], (TOKENS, KVH, HD), 1.0, 6.0, ((0, 32),)),
        "grad_out": normal_values(own_keys[3], (TOKENS, H, HD), 1.0, 6.0, ((0, 32),)),
        "doc_lengths": draw_doc_lengths(jax.random.fold_in(jax.random.fold_in(keys[5], part), 71), part),
    }


def segment_ids(doc_lengths, seq_total):
    doc_ends = jnp.cumsum(doc_lengths)
    positions = jnp.arange(seq_total, dtype=jnp.int32)
    return jnp.sum((positions[:, None] >= doc_ends[None, :]).astype(jnp.int32), axis=1)


def contract(left, right, dims):
    return lax.dot_general(left, right, (dims, ((), ())), preferred_element_type=jnp.float32)


def group_pass(query_heads, grad_heads, key_rows, value_rows, segment):
    seq_total, head_count, head_width = query_heads.shape
    scale = head_width ** -0.5
    block_rows = math.gcd(seq_total, 512)
    window = block_rows + seq_total // 4
    positions = jnp.arange(seq_total, dtype=jnp.int32)
    key_grad = jnp.zeros((seq_total, head_width), jnp.float32)
    value_grad = jnp.zeros((seq_total, head_width), jnp.float32)
    out_blocks = []
    grad_blocks = []
    for block_index in range(seq_total // block_rows):
        start_row = block_index * block_rows
        stop_row = start_row + block_rows
        key_low = max(0, stop_row - window)
        query_block = query_heads[start_row:stop_row].reshape(block_rows * head_count, head_width)
        cotangent = grad_heads[start_row:stop_row].reshape(block_rows * head_count, head_width)
        key_block = key_rows[key_low:stop_row]
        value_block = value_rows[key_low:stop_row]
        query_pos = jnp.repeat(positions[start_row:stop_row], head_count)
        query_seg = jnp.repeat(segment[start_row:stop_row], head_count)
        allowed = (query_seg[:, None] == segment[None, key_low:stop_row]) & (positions[None, key_low:stop_row] <= query_pos[:, None])
        scores = contract(query_block, key_block, ((1,), (1,))) * scale
        scores = jnp.where(allowed, scores, -jnp.inf)
        row_max = jnp.max(scores, axis=1)
        exponent = jnp.exp(scores - row_max[:, None])
        totals = jnp.sum(exponent, axis=1)
        attended_block = (contract(exponent.astype(jnp.bfloat16), value_block, ((1,), (0,))) / totals[:, None]).astype(jnp.bfloat16)
        probs = exponent / totals[:, None]
        dprobs = contract(cotangent, value_block, ((1,), (1,)))
        delta = jnp.sum(cotangent.astype(jnp.float32) * attended_block.astype(jnp.float32), axis=1)
        dscores = (probs * (dprobs - delta[:, None])).astype(jnp.bfloat16)
        grad_block = (scale * contract(dscores, key_block, ((1,), (0,)))).astype(jnp.bfloat16)
        key_grad = key_grad.at[key_low:stop_row].add(scale * contract(dscores, query_block, ((0,), (0,))))
        value_grad = value_grad.at[key_low:stop_row].add(contract(probs.astype(jnp.bfloat16), cotangent, ((0,), (0,))))
        out_blocks.append(attended_block.reshape(block_rows, head_count, head_width))
        grad_blocks.append(grad_block.reshape(block_rows, head_count, head_width))
    return jnp.concatenate(out_blocks, axis=0), jnp.concatenate(grad_blocks, axis=0), key_grad, value_grad


def reference(queries, key_states, value_states, grad_out, doc_lengths):
    groups = H // KVH
    segment = segment_ids(doc_lengths, TOKENS)
    query_groups = queries.reshape(TOKENS, KVH, groups, HD).transpose(1, 0, 2, 3)
    grad_groups = grad_out.reshape(TOKENS, KVH, groups, HD).transpose(1, 0, 2, 3)
    key_heads = key_states.transpose(1, 0, 2)
    value_heads = value_states.transpose(1, 0, 2)

    def per_group(operands):
        return group_pass(operands[0], operands[1], operands[2], operands[3], segment)

    attended, grad_queries, key_grad, value_grad = lax.map(per_group, (query_groups, grad_groups, key_heads, value_heads))
    attended = attended.transpose(1, 0, 2, 3).reshape(TOKENS, H, HD)
    grad_queries = grad_queries.transpose(1, 0, 2, 3).reshape(TOKENS, H, HD)
    grad_keys = key_grad.transpose(1, 0, 2).astype(jnp.bfloat16)
    grad_values = value_grad.transpose(1, 0, 2).astype(jnp.bfloat16)
    return attended, grad_queries, grad_keys, grad_values
```

```python
import functools

import jax
import jax.numpy as jnp
from jax import lax
from jax.experimental import pallas as pl
from jax.experimental.pallas import tpu as pltpu
from jax.sharding import PartitionSpec as P

BLOCK = 128
CHUNK = 256
WINDOW = 2048
LOG2E = 1.4426950408889634
MASKED = -1e30

NT = (((1,), (1,)), ((), ()))
NN = (((1,), (0,)), ((), ()))
TN = (((0,), (0,)), ((), ()))


def dot(a, b, dims):
    return lax.dot_general(a, b, dims, preferred_element_type=jnp.float32)


def attend_block(q, do, bounds, first, last, k_win, v_win, s_scr, dk_acc, dv_acc):
    rows, width = q.shape
    scale = width**-0.5
    low, high = bounds
    key_iota = lax.broadcasted_iota(jnp.int32, (CHUNK, rows), 0)

    def scores(c, top):
        at = pl.ds(pl.multiple_of(c * CHUNK, CHUNK), CHUNK)
        s = dot(k_win[at, :], q, NT)
        pos = key_iota + c * CHUNK
        s = jnp.where((pos >= low) & (pos <= high), s, MASKED)
        s_scr[at, :] = s
        return jnp.maximum(top, jnp.max(s.reshape(CHUNK // 8, 8, rows), axis=0))

    top = lax.fori_loop(first, last, scores, jnp.full((8, rows), MASKED, jnp.float32))
    top = jnp.max(top, axis=0, keepdims=True)

    def forward(c, carry):
        total, att = carry
        at = pl.ds(pl.multiple_of(c * CHUNK, CHUNK), CHUNK)
        e = jnp.exp2((s_scr[at, :] - top) * (scale * LOG2E))
        s_scr[at, :] = e
        total = total + jnp.sum(e.reshape(CHUNK // 8, 8, rows), axis=0)
        att = att + dot(v_win[at, :], e.astype(jnp.bfloat16), TN)
        return total, att

    total, att = lax.fori_loop(
        first, last, forward, (jnp.zeros((8, rows), jnp.float32), jnp.zeros((width, rows), jnp.float32))
    )
    inv = 1.0 / jnp.sum(total, axis=0, keepdims=True)
    att = (att * inv).astype(jnp.bfloat16)
    att_rows = att.astype(jnp.float32).T
    delta = jnp.sum(att.astype(jnp.float32) * do.astype(jnp.float32).T, axis=0, keepdims=True)

    def backward(c, dq):
        at = pl.ds(pl.multiple_of(c * CHUNK, CHUNK), CHUNK)
        k = k_win[at, :]
        p = s_scr[at, :] * inv
        dp = dot(v_win[at, :], do, NT)
        ds = (p * (dp - delta)).astype(jnp.bfloat16)
        dv_acc[at, :] += dot(p.astype(jnp.bfloat16), do, NN)
        dk_acc[at, :] += dot(ds, q, NN)
        return dq + dot(k, ds, TN)

    dq = lax.fori_loop(first, last, backward, jnp.zeros((width, rows), jnp.float32))
    return att_rows.astype(jnp.bfloat16), (dq * scale).T.astype(jnp.bfloat16)


def attend_kernel(meta, q_own, q_got, do_own, do_got, bounds, *refs):
    keys = refs[:10]
    att_own, att_send, dq_own, dq_send = refs[10:14]
    grads = refs[14:22]
    k_win, v_win, s_scr, dk_acc, dv_acc = refs[22:]
    x = meta[0]

    def place(row, half, shift):
        return pl.ds(pl.multiple_of((row * 8 + half * 4 + lax.rem(x + shift, 4)) * BLOCK, BLOCK), BLOCK)

    for row in range(2):
        own, plus, minus, two_a, two_b = keys[row * 5 : row * 5 + 5]
        for half in range(2):
            for ref, shift in ((own, 0), (plus, 3), (minus, 1)):
                k_win[place(row, half, shift), :] = ref[half, 0, 0]
                v_win[place(row, half, shift), :] = ref[half, 1, 0]
            ref = (two_a, two_b)[half]
            k_win[place(row, half, 2), :] = ref[0, 0]
            v_win[place(row, half, 2), :] = ref[1, 0]
    dk_acc[...] = jnp.zeros_like(dk_acc)
    dv_acc[...] = jnp.zeros_like(dv_acc)

    for slot, (q_ref, do_ref, att_ref, dq_ref) in enumerate(
        ((q_own, do_own, att_own, dq_own), (q_got, do_got, att_send, dq_send))
    ):
        shape = (q_ref.shape[0] * q_ref.shape[2], q_ref.shape[3])
        q = q_ref[:, 0].reshape(shape)
        do = do_ref[:, 0].reshape(shape)
        limits = (bounds[2 * slot : 2 * slot + 1, :], bounds[2 * slot + 1 : 2 * slot + 2, :])
        att, dq = attend_block(
            q, do, limits, meta[2 + 2 * slot], meta[3 + 2 * slot], k_win, v_win, s_scr, dk_acc, dv_acc
        )
        att_ref[:, 0] = att.reshape(BLOCK, 8, shape[1])
        dq_ref[:, 0] = dq.reshape(BLOCK, 8, shape[1])

    scale = q_own.shape[3] ** -0.5
    for row in range(2):
        for shift in range(4):
            out = grads[row * 4 + shift]
            for half in range(2):
                at = place(row, half, shift)
                out[half, 0, 0] = (dk_acc[at, :] * scale).astype(jnp.bfloat16)
                out[half, 1, 0] = dv_acc[at, :].astype(jnp.bfloat16)


def attend(meta, q4, q_got, do4, do_got, bounds, keys):
    groups = q_got.shape[1]
    rows = BLOCK * 8
    width = q4.shape[3]
    full = (BLOCK, 1, 8, width)
    own = pl.BlockSpec(full, lambda g, m: (0, g + groups * m[1], 0, 0))
    got = pl.BlockSpec(full, lambda g, m: (0, g, 0, 0))
    pair = pl.BlockSpec((2, 2, 1, BLOCK, width), lambda g, m: (0, 0, g, 0, 0))
    one = pl.BlockSpec((2, 1, BLOCK, width), lambda g, m: (0, g, 0, 0))
    whole = jax.ShapeDtypeStruct(q4.shape, jnp.bfloat16)
    part = jax.ShapeDtypeStruct(q_got.shape, jnp.bfloat16)
    grad = jax.ShapeDtypeStruct((2, 2, groups, BLOCK, width), jnp.bfloat16)
    return pl.pallas_call(
        attend_kernel,
        grid_spec=pltpu.PrefetchScalarGridSpec(
            num_scalar_prefetch=1,
            grid=(groups,),
            in_specs=[own, got, own, got, pl.BlockSpec((4, rows), lambda g, m: (0, 0))]
            + [pair, pair, pair, one, one] * 2,
            out_specs=[own, got, own, got] + [pair] * 8,
            scratch_shapes=[
                pltpu.VMEM((WINDOW, width), jnp.bfloat16),
                pltpu.VMEM((WINDOW, width), jnp.bfloat16),
                pltpu.VMEM((WINDOW, rows), jnp.float32),
                pltpu.VMEM((WINDOW, width), jnp.float32),
                pltpu.VMEM((WINDOW, width), jnp.float32),
            ],
        ),
        out_shape=[whole, part, whole, part] + [grad] * 8,
        compiler_params=pltpu.CompilerParams(vmem_limit_bytes=56 * 1024 * 1024),
        cost_estimate=pl.CostEstimate(flops=10_000_000_000, bytes_accessed=24_000_000, transcendentals=8_000_000),
        name="attend",
    )(meta, q4, q_got, do4, do_got, bounds, *keys)


def shards(queries, key_states, value_states, grad_out, doc_lengths):
    tokens, heads, width = queries.shape
    kv_heads = key_states.shape[1]
    per = heads // kv_heads
    groups = kv_heads // 2
    ctx = lax.axis_index("ctx")
    x = lax.axis_index("tensor")
    y, core = ctx // 2, ctx % 2

    swap = [(i, i ^ 1) for i in range(8)]
    up = [(i, i + 2) for i in range(6)]
    down = [(i + 2, i) for i in range(6)]
    right = [(i, (i + 1) % 4) for i in range(4)]
    left = [(i, (i + 3) % 4) for i in range(4)]

    kv = jnp.stack([key_states, value_states]).transpose(0, 2, 1, 3).reshape(2, 2, groups, tokens, width)
    kv_own = lax.dynamic_index_in_dim(kv, core, 1, keepdims=False)
    kv_send = lax.dynamic_index_in_dim(kv, 1 - core, 1, keepdims=False)
    kv_got = lax.ppermute(kv_send, "ctx", swap)
    row = jnp.stack([jnp.where(core == 0, kv_own, kv_got), jnp.where(core == 0, kv_got, kv_own)])

    def spread(r):
        plus = lax.ppermute(r, "tensor", right)
        minus = lax.ppermute(r, "tensor", left)
        return [r, plus, minus, lax.ppermute(plus[0], "tensor", right), lax.ppermute(minus[1], "tensor", left)]

    before = lax.ppermute(row, "ctx", up)
    here = spread(row)
    earlier = spread(before)

    q4 = queries.reshape(tokens, kv_heads, per, width)
    do4 = grad_out.reshape(tokens, kv_heads, per, width)
    q_got = lax.ppermute(lax.dynamic_slice_in_dim(q4, groups * (1 - core), groups, 1), "ctx", swap)
    do_got = lax.ppermute(lax.dynamic_slice_in_dim(do4, groups * (1 - core), groups, 1), "ctx", swap)

    base = (y - 1) * 1024
    ends = jnp.cumsum(doc_lengths)

    def limits(half):
        pos = y * 1024 + half * 512 + x * tokens + jnp.arange(tokens, dtype=jnp.int32)
        start = jnp.max(jnp.where(ends[None, :] <= pos[:, None], ends[None, :], 0), axis=1)
        return start - base, pos - base

    low0, high0 = limits(core)
    low1, high1 = limits(1 - core)
    bounds = jnp.repeat(jnp.stack([low0, high0, low1, high1]), per, axis=1)
    meta = jnp.stack(
        [x, core, low0[0] // CHUNK, high0[-1] // CHUNK + 1, low1[0] // CHUNK, high1[-1] // CHUNK + 1]
    ).astype(jnp.int32)

    att, att_send, dq, dq_send, *grads = attend(meta, q4, q_got, do4, do_got, bounds, earlier + here)

    def settle(full, send):
        got = lax.ppermute(send, "ctx", swap)
        return lax.dynamic_update_slice_in_dim(full, got, groups * (1 - core), 1).reshape(tokens, heads, width)

    def add(*terms):
        return sum(t.astype(jnp.float32) for t in terms)

    def collect(parts):
        own, plus, two, minus = parts
        two_a = lax.ppermute(two[0], "tensor", right)
        two_b = lax.ppermute(two[1], "tensor", left)
        plus = jnp.stack([add(plus[0], two_a).astype(jnp.bfloat16), plus[1]])
        minus = jnp.stack([minus[0], add(minus[1], two_b).astype(jnp.bfloat16)])
        return add(own, lax.ppermute(plus, "tensor", right), lax.ppermute(minus, "tensor", left))

    back = lax.ppermute(collect(grads[:4]).astype(jnp.bfloat16), "ctx", down)
    both = add(collect(grads[4:]), back).astype(jnp.bfloat16)
    mine = lax.dynamic_index_in_dim(both, core, 0, keepdims=False)
    theirs = lax.ppermute(lax.dynamic_index_in_dim(both, 1 - core, 0, keepdims=False), "ctx", swap)
    kv_grad = jnp.stack([jnp.where(core == 0, mine, theirs), jnp.where(core == 0, theirs, mine)], axis=1)
    kv_grad = kv_grad.reshape(2, kv_heads, tokens, width).transpose(0, 2, 1, 3)
    return settle(att, att_send), settle(dq, dq_send), kv_grad[0], kv_grad[1]


def solution(mesh):
    placed = P(("dp", "ctx", "tensor"), None, None)
    return jax.shard_map(
        shards,
        mesh=mesh,
        in_specs=(placed, placed, placed, placed, P("dp")),
        out_specs=(placed, placed, placed, placed),
        check_vma=False,
    )
```

```python
import functools

import jax
import jax.numpy as jnp
from jax import lax
from jax.experimental import pallas as pl
from jax.experimental.pallas import tpu as pltpu
from jax.sharding import PartitionSpec as P

BLOCK = 128
TILE = 512
CHUNK = 256
PARTS = ((0, 2), (2, 2))
WINDOW = 2048
STEPS = 5
COST = 15_000_000_000
LOG2E = 1.4426950408889634
MASKED = -1e30

NT = (((1,), (1,)), ((), ()))
NN = (((1,), (0,)), ((), ()))
TN = (((0,), (0,)), ((), ()))


def dot(a, b, dims):
    return lax.dot_general(a, b, dims, preferred_element_type=jnp.float32)


def attend_kernel(start, lengths, q4, q_got, do4, do_got, early, others, *refs):
    att_own, att_send, dq_own, dq_send, early_grad, others_grad = refs[-28:-22]
    (
        k_win,
        v_win,
        e_scr,
        dp_scr,
        top_scr,
        total_scr,
        att_acc,
        dq_acc,
        dk_acc,
        dv_acc,
        q_scr,
        do_scr,
        in_buf,
        out_buf,
        early_buf,
        others_buf,
        early_out,
        others_out,
        in_sem,
        out_sem,
        key_sem,
        grad_sem,
    ) = refs[-22:]
    x = lax.axis_index("tensor")
    ctx = lax.axis_index("ctx")
    y, core = ctx // 2, ctx % 2
    ends = [lengths[0]]
    for i in range(1, lengths.shape[0]):
        ends.append(ends[-1] + lengths[i])

    def document(pos):
        begin = jnp.zeros_like(pos)
        for last in ends:
            begin = jnp.where(last <= pos, last, begin)
        return begin

    groups, rows, width = q_scr.shape
    ours = pl.ds(q_got.shape[1] * core + start, groups)
    here_got = pl.ds(start, groups)

    def read(slot, which):
        source = ((q4, do4), (q_got, do_got))[slot][which].at[:, (ours, here_got)[slot]]
        return pltpu.make_async_copy(source, in_buf.at[slot, which], in_sem.at[slot, which])

    def write(slot, which):
        target = ((att_own, dq_own), (att_send, dq_send))[slot][which]
        target = target.at[:, ours] if slot == 0 else target
        return pltpu.make_async_copy(out_buf.at[slot, which], target, out_sem.at[slot, which])

    key_reads = [
        pltpu.make_async_copy(others, others_buf, key_sem.at[0]),
        pltpu.make_async_copy(early, early_buf, key_sem.at[1]),
    ]
    for copy in key_reads:
        copy.start()
    for slot in range(2):
        for which in range(2):
            read(slot, which).start()
    scale = width**-0.5
    power = scale * LOG2E

    def pieces(early, others):
        found = [(early, (), x)]
        for d in range(4):
            found.append((others, (d, 0), 8 + d))
            found.append((others, (d, 1), 4 + d))
            found.append((others, (d, 2), jnp.where(d > x, d, 12 + d)))
        return [(ref, index, pl.ds(pl.multiple_of((block + 1) * BLOCK, BLOCK), BLOCK)) for ref, index, block in found]

    k_win[...] = jnp.zeros_like(k_win)
    v_win[...] = jnp.zeros_like(v_win)
    dk_acc[...] = jnp.zeros_like(dk_acc)
    dv_acc[...] = jnp.zeros_like(dv_acc)
    for copy in key_reads:
        copy.wait()
    for ref, index, at in pieces(early_buf, others_buf):
        for g in range(groups):
            k_win[g, at, :] = ref[(*index, 0, g)]
            v_win[g, at, :] = ref[(*index, 1, g)]

    @pl.loop(0, 2)
    def _(slot):
        for which, scr in enumerate((q_scr, do_scr)):
            pltpu.make_async_copy(q_got.at[:, here_got], in_buf.at[slot, which], in_sem.at[slot, which]).wait()
            for g in range(groups):
                scr[g] = in_buf[slot, which, :, g].reshape(rows, width)
        base = (y - 1) * (WINDOW // 2)
        begin = (8 + 4 * jnp.where(slot == 0, core, 1 - core) + x) * BLOCK
        end = begin + BLOCK
        count = (end - 1 - (document(base + begin) - base)) // CHUNK + 1
        last_low = document(base + end - 1) - base
        token = begin + lax.broadcasted_iota(jnp.int32, (1, rows), 1) // (rows // BLOCK)
        low = document(base + token) - base
        span = token - low
        top_scr[STEPS] = jnp.full((groups, 1, rows), MASKED, jnp.float32)
        total_scr[...] = jnp.zeros_like(total_scr)
        att_acc[...] = jnp.zeros_like(att_acc)
        dq_acc[...] = jnp.zeros_like(dq_acc)

        def keys_at(i):
            return pl.ds(pl.multiple_of(end + BLOCK - (i + 1) * CHUNK, BLOCK), CHUNK)

        def forward(i, inner):
            here = keys_at(i)
            tiles = [(g, slice(t, t + TILE)) for g in range(groups) for t in range(0, rows, TILE)]
            offset = lax.broadcasted_iota(jnp.int32, (CHUNK, TILE), 0) + (end - (i + 1) * CHUNK)

            def score(g, t):
                return dot(k_win[g, here, :], q_scr[g, t, :], NT)

            ahead = score(*tiles[0])
            for n, (g, t) in enumerate(tiles):
                s = ahead
                if n + 1 < len(tiles):
                    ahead = score(*tiles[n + 1])
                v = v_win[g, here, :]
                dp_scr[g, i, :, t] = dot(v, do_scr[g, t, :], NT)
                if not inner:
                    past = (offset - low[:, t]).astype(jnp.uint32)
                    s = jnp.where(past <= span[:, t].astype(jnp.uint32), s, MASKED)
                old = top_scr[STEPS, g, :, t]
                top = jnp.maximum(old, jnp.max(s, axis=0, keepdims=True))
                e = jnp.exp2((s - top) * power)
                fade = jnp.exp2((old - top) * power)
                e_scr[g, i, :, t] = e
                top_scr[i, g, :, t] = top
                top_scr[STEPS, g, :, t] = top
                total_scr[g, :, t] = total_scr[g, :, t] * fade + jnp.sum(e, axis=0, keepdims=True)
                att_acc[g, :, t] = att_acc[g, :, t] * fade + dot(v, e.astype(jnp.bfloat16), TN)

        @pl.loop(0, count)
        def _(i):
            inner = (i > 0) & (end - (i + 1) * CHUNK >= last_low)

            @pl.when(inner)
            def _():
                forward(i, True)

            @pl.when(jnp.logical_not(inner))
            def _():
                forward(i, False)

        inverse, delta = [], []
        for g in range(groups):
            inv = 1.0 / total_scr[g]
            att = (att_acc[g] * inv).astype(jnp.bfloat16)
            out_buf[slot, 0, :, g] = att.T.reshape(BLOCK, 8, width)
            do_t = do_scr[g].T.astype(jnp.float32)
            inverse.append(inv)
            delta.append(jnp.sum(att.astype(jnp.float32) * do_t, axis=0, keepdims=True))

        @pl.loop(0, count)
        def _(i):
            for g in range(groups):
                here = keys_at(i)
                p = e_scr[g, i] * (jnp.exp2((top_scr[i, g] - top_scr[STEPS, g]) * power) * inverse[g])
                dp = dp_scr[g, i]
                ds = (p * (dp - delta[g])).astype(jnp.bfloat16)
                dv_acc[g, here, :] += dot(p.astype(jnp.bfloat16), do_scr[g], NN)
                dk_acc[g, here, :] += dot(ds, q_scr[g], NN)
                dq_acc[g] += dot(k_win[g, here, :], ds, TN)

        for g in range(groups):
            out_buf[slot, 1, :, g] = (dq_acc[g] * scale).astype(jnp.bfloat16).T.reshape(BLOCK, 8, width)
        for which in range(2):

            @pl.when(slot == 0)
            def _():
                write(0, which).start()

            @pl.when(slot == 1)
            def _():
                write(1, which).start()

    for ref, index, at in pieces(early_out, others_out):
        for g in range(groups):
            ref[(*index, 0, g)] = (dk_acc[g, at, :] * scale).astype(ref.dtype)
            ref[(*index, 1, g)] = dv_acc[g, at, :].astype(ref.dtype)
    grad_writes = [
        pltpu.make_async_copy(others_out, others_grad, grad_sem.at[0]),
        pltpu.make_async_copy(early_out, early_grad, grad_sem.at[1]),
    ]
    for copy in grad_writes:
        copy.start()
    for slot in range(2):
        for which in range(2):
            write(slot, which).wait()
    for copy in grad_writes:
        copy.wait()


def attend(start, lengths, q4, q_got, do4, do_got, early, others, filled):
    groups = others.shape[3]
    rows = BLOCK * 8
    width = q4.shape[3]
    full = (BLOCK, groups, 8, width)
    away = pl.BlockSpec(memory_space=pl.ANY)
    shapes = [(2, groups, BLOCK, width), (4, 3, 2, groups, BLOCK, width)]
    whole = jax.ShapeDtypeStruct(q4.shape, jnp.bfloat16)
    piece = jax.ShapeDtypeStruct(full, jnp.bfloat16)
    return pl.pallas_call(
        functools.partial(attend_kernel, start),
        grid_spec=pltpu.PrefetchScalarGridSpec(
            num_scalar_prefetch=1,
            grid=(1,),
            in_specs=[away] * (6 + len(filled)),
            out_specs=[away] * 6,
            scratch_shapes=[
                pltpu.VMEM((groups, WINDOW + BLOCK, width), jnp.bfloat16),
                pltpu.VMEM((groups, WINDOW + BLOCK, width), jnp.bfloat16),
                pltpu.VMEM((groups, STEPS, CHUNK, rows), jnp.float32),
                pltpu.VMEM((groups, STEPS, CHUNK, rows), jnp.float32),
                pltpu.VMEM((STEPS + 1, groups, 1, rows), jnp.float32),
                pltpu.VMEM((groups, 1, rows), jnp.float32),
                pltpu.VMEM((groups, width, rows), jnp.float32),
                pltpu.VMEM((groups, width, rows), jnp.float32),
                pltpu.VMEM((groups, WINDOW + BLOCK, width), jnp.float32),
                pltpu.VMEM((groups, WINDOW + BLOCK, width), jnp.float32),
                pltpu.VMEM((groups, rows, width), jnp.bfloat16),
                pltpu.VMEM((groups, rows, width), jnp.bfloat16),
                pltpu.VMEM((2, 2, *full), jnp.bfloat16),
                pltpu.VMEM((2, 2, *full), jnp.bfloat16),
            ]
            + [pltpu.VMEM(a, jnp.bfloat16) for a in shapes * 2]
            + [
                pltpu.SemaphoreType.DMA((2, 2)),
                pltpu.SemaphoreType.DMA((2, 2)),
                pltpu.SemaphoreType.DMA((2,)),
                pltpu.SemaphoreType.DMA((2,)),
            ],
        ),
        out_shape=[whole, piece, whole, piece]
        + [jax.ShapeDtypeStruct(a, jnp.bfloat16) for a in shapes],
        input_output_aliases={7: 0, 8: 2} if filled else {},
        compiler_params=pltpu.CompilerParams(vmem_limit_bytes=56 * 1024 * 1024),
        cost_estimate=pl.CostEstimate(
            flops=COST * groups, bytes_accessed=6_000_000 * groups, transcendentals=2_000_000 * groups
        ),
        name="attend",
    )(lengths, q4, q_got, do4, do_got, early, others, *filled)


def shards(queries, key_states, value_states, grad_out, doc_lengths):
    tokens, heads, width = queries.shape
    kv_heads = key_states.shape[1]
    per = heads // kv_heads
    groups = kv_heads // 2
    lead = PARTS[0][1]
    ctx = lax.axis_index("ctx")
    x = lax.axis_index("tensor")
    core = ctx % 2

    swap = [(i, i ^ 1) for i in range(8)]
    up = [(i, i + 2) for i in range(6)]
    down = [(i + 2, i) for i in range(6)]

    kv = jnp.stack([key_states, value_states]).transpose(0, 2, 1, 3).reshape(2, 2, groups, tokens, width)
    kv_own = lax.dynamic_index_in_dim(kv, core, 1, keepdims=False)
    kv_send = lax.dynamic_index_in_dim(kv, 1 - core, 1, keepdims=False)
    kv_got = lax.ppermute(kv_send, "ctx", swap)
    row = jnp.stack([jnp.where(core == 0, kv_own, kv_got), jnp.where(core == 0, kv_got, kv_own)])

    q4 = queries.reshape(tokens, kv_heads, per, width)
    do4 = grad_out.reshape(tokens, kv_heads, per, width)
    q_send = lax.dynamic_slice_in_dim(q4, groups * (1 - core), groups, 1)
    do_send = lax.dynamic_slice_in_dim(do4, groups * (1 - core), groups, 1)

    before = [lax.ppermute(row[:, :, :lead], "ctx", up), lax.ppermute(row[:, :, lead:], "ctx", up)]
    q_got = lax.ppermute(q_send, "ctx", swap)
    do_got = lax.ppermute(do_send, "ctx", swap)
    earlier, others = [], []
    for start, size in PARTS:
        own = row[:, :, start : start + size]
        old = before[0] if start == 0 else before[1][:, :, start - lead : start - lead + size]
        one = jnp.stack([jnp.stack([own[0], old[1], jnp.where(d < x, old[0], own[1])]) for d in range(4)])
        earlier.append(old[0])
        others.append(lax.all_to_all(one, "tensor", split_axis=0, concat_axis=0, tiled=True))

    filled, sent, sums = [], [], []
    for (start, _), old, other in zip(PARTS, earlier, others):
        att, att_send, dq, dq_send, early, partial = attend(
            start, doc_lengths, q4, q_got, do4, do_got, old, other, filled
        )
        filled = [att, dq]
        sent.append([lax.ppermute(att_send, "ctx", swap), lax.ppermute(dq_send, "ctx", swap)])
        back = lax.all_to_all(partial, "tensor", split_axis=0, concat_axis=0, tiled=True).astype(jnp.float32)
        first, late = jnp.sum(back[:, 0], axis=0), jnp.sum(back[:, 1], axis=0)
        early = early.astype(jnp.float32)
        second = jnp.zeros_like(early)
        for d in range(4):
            early = early + jnp.where(d < x, back[d, 2], 0)
            second = second + jnp.where(d < x, 0, back[d, 2])
        sums.append((first, second, jnp.stack([early, late]).astype(jnp.bfloat16)))

    def settle(full, index):
        for (start, _), got in zip(PARTS, sent):
            full = lax.dynamic_update_slice_in_dim(full, got[index], groups * (1 - core) + start, 1)
        return full.reshape(tokens, heads, width)

    attended, grad_queries = settle(filled[0], 0), settle(filled[1], 1)

    def finish(first, second, send):
        got = lax.ppermute(send, "ctx", down).astype(jnp.float32)
        both = jnp.stack([first + got[0], second + got[1]]).astype(jnp.bfloat16)
        mine = lax.dynamic_index_in_dim(both, core, 0, keepdims=False)
        theirs = lax.ppermute(lax.dynamic_index_in_dim(both, 1 - core, 0, keepdims=False), "ctx", swap)
        return jnp.where(core == 0, mine, theirs), jnp.where(core == 0, theirs, mine)

    head = [jnp.concatenate(t, axis=-3) for t in zip(*sums[:-1])]
    first, second, send = sums[-1]
    send, attended, grad_queries = lax.optimization_barrier((send, attended, grad_queries))
    done, at = {}, 0
    whole = finish(*head)
    for start, size in PARTS[:-1]:
        done[start] = [h[:, at : at + size] for h in whole]
        at += size
    done[PARTS[-1][0]] = finish(first, second, send)
    kv_grad = jnp.concatenate([done[start][core_half] for core_half in range(2) for start in sorted(done)], axis=1)
    kv_grad = kv_grad.transpose(0, 2, 1, 3)
    return attended, grad_queries, kv_grad[0], kv_grad[1]


def solution(mesh):
    placed = P(("dp", "ctx", "tensor"), None, None)
    return jax.shard_map(
        shards,
        mesh=mesh,
        in_specs=(placed, placed, placed, placed, P("dp")),
        out_specs=(placed, placed, placed, placed),
        check_vma=False,
    )
```

```python
import functools

import jax
import jax.numpy as jnp
from jax import lax
from jax.experimental import pallas as pl
from jax.experimental.pallas import tpu as pltpu
from jax.sharding import PartitionSpec as P

BLOCK = 128
SUB = 32
TILE = 512
CHUNK = 256
PARTS = ((0, 2), (2, 2))
WINDOW = 2048
STEPS = 5
COST = 15_000_000_000
LOG2E = 1.4426950408889634
MASKED = -1e30

NT = (((1,), (1,)), ((), ()))
NN = (((1,), (0,)), ((), ()))
TN = (((0,), (0,)), ((), ()))


def dot(a, b, dims):
    return lax.dot_general(a, b, dims, preferred_element_type=jnp.float32)


def attend_kernel(start, keys, last, lengths, q4, q_got, do4, do_got, *refs):
    results = 5 if last else 2
    *refs, in_sem, out_sem, key_sem, grad_sem = refs
    key_refs = refs[:keys]
    refs, grad_bufs = refs[:-results], refs[-results:]
    refs, key_bufs = refs[:-keys], refs[-keys:]
    (
        k_win,
        v_win,
        e_scr,
        s_scr,
        dp_scr,
        top_scr,
        total_scr,
        att_acc,
        dq_acc,
        dk_acc,
        dv_acc,
        q_scr,
        do_scr,
        in_buf,
        out_buf,
    ) = refs[-15:]
    att_own, att_send, dq_own, dq_send, *grad_refs = refs[-15 - 4 - results : -15]
    x = lax.axis_index("tensor")
    ctx = lax.axis_index("ctx")
    y, core = ctx // 2, ctx % 2
    ends = [lengths[0]]
    for i in range(1, lengths.shape[0]):
        ends.append(ends[-1] + lengths[i])

    def document(pos):
        begin = jnp.zeros_like(pos)
        for last in ends:
            begin = jnp.where(last <= pos, last, begin)
        return begin

    groups, rows, width = q_scr.shape
    ours = pl.ds(q_got.shape[1] * core + start, groups)
    here_got = pl.ds(start, groups)

    def read(slot, which):
        source = ((q4, do4), (q_got, do_got))[slot][which].at[:, (ours, here_got)[slot]]
        return pltpu.make_async_copy(source, in_buf.at[slot, which], in_sem.at[slot, which])

    def write(slot, which):
        target = ((att_own, dq_own), (att_send, dq_send))[slot][which]
        target = target.at[:, ours] if slot == 0 else target
        return pltpu.make_async_copy(out_buf.at[slot, which], target, out_sem.at[slot, which])

    key_reads = [
        pltpu.make_async_copy(ref, buf, key_sem.at[i]) for i, (ref, buf) in enumerate(zip(key_refs, key_bufs))
    ]
    for copy in key_reads:
        copy.start()
    for slot in range(2):
        for which in range(2):
            read(slot, which).start()
    scale = width**-0.5
    power = scale * LOG2E

    def place(block):
        return pl.ds(pl.multiple_of((block + 1) * BLOCK, BLOCK), BLOCK)

    def pieces(*bufs):
        found = []
        if len(bufs) == 5:
            before, own, *around = bufs
            for half in range(2):
                found.append((own, (half,), 8 + 4 * half + x))
                found.append((before, (half,), 4 * half + x))
            for shift, ref in enumerate(around, 1):
                source = lax.rem(x + 4 - shift, 4)
                found.append((ref, (0,), 4 + source))
                found.append((ref, (1,), jnp.where(source > x, source, 12 + source)))
                found.append((ref, (2,), 8 + source))
            return [(ref, index, place(block)) for ref, index, block in found]
        early, others, *around = bufs
        for shift, ref in enumerate(around):
            found.append((ref, (), 8 + lax.rem(x + 4 - shift, 4)))
        if not around:
            found = [(others, (d, 2), 8 + d) for d in range(4)]
        found.append((early, (), x))
        for d in range(4):
            found.append((others, (d, 0), 4 + d))
            found.append((others, (d, 1), jnp.where(d > x, d, 12 + d)))
        return [(ref, index, place(block)) for ref, index, block in found]

    k_win[...] = jnp.zeros_like(k_win)
    v_win[...] = jnp.zeros_like(v_win)
    dk_acc[...] = jnp.zeros_like(dk_acc)
    dv_acc[...] = jnp.zeros_like(dv_acc)
    for copy in key_reads:
        copy.wait()
    for ref, index, at in pieces(*key_bufs):
        for g in range(groups):
            k_win[g, at, :] = ref[(*index, 0, g)]
            v_win[g, at, :] = ref[(*index, 1, g)]

    @pl.loop(0, 2)
    def _(slot):
        for which, scr in enumerate((q_scr, do_scr)):
            pltpu.make_async_copy(q_got.at[:, here_got], in_buf.at[slot, which], in_sem.at[slot, which]).wait()
            for g in range(groups):
                scr[g] = in_buf[slot, which, :, g].reshape(rows, width)
        base = (y - 1) * (WINDOW // 2)
        begin = (8 + 4 * jnp.where(slot == 0, core, 1 - core) + x) * BLOCK
        end = begin + BLOCK
        count = (end - 1 - (document(base + begin) - base)) // CHUNK + 1
        last_low = document(base + end - 1) - base
        token = begin + lax.broadcasted_iota(jnp.int32, (1, rows), 1) // (rows // BLOCK)
        low = document(base + token) - base
        span = token - low
        top_scr[STEPS] = jnp.full((groups, 1, rows), MASKED, jnp.float32)
        total_scr[...] = jnp.zeros_like(total_scr)
        att_acc[...] = jnp.zeros_like(att_acc)
        dq_acc[...] = jnp.zeros_like(dq_acc)

        def keys_at(i):
            return pl.ds(pl.multiple_of(end + BLOCK - (i + 1) * CHUNK, BLOCK), CHUNK)

        def forward(i, inner):
            here = keys_at(i)
            tiles = [(g, slice(t, t + TILE)) for g in range(groups) for t in range(0, rows, TILE)]
            offset = lax.broadcasted_iota(jnp.int32, (CHUNK, TILE), 0) + (end - (i + 1) * CHUNK)

            def score(n):
                g, t = tiles[n]
                s = dot(k_win[g, here, :], q_scr[g, t, :], NT)
                if not inner:
                    past = (offset - low[:, t]).astype(jnp.uint32)
                    s = jnp.where(past <= span[:, t].astype(jnp.uint32), s, MASKED)
                s_scr[n % 2] = s
                return jnp.max(s, axis=0, keepdims=True)

            ahead = score(0)
            for n, (g, t) in enumerate(tiles):
                high = ahead
                if n + 1 < len(tiles):
                    ahead = score(n + 1)
                v = v_win[g, here, :]
                dp_scr[g, i, :, t] = dot(v, do_scr[g, t, :], NT)
                old = top_scr[STEPS, g, :, t]
                top = jnp.maximum(old, high)
                fade = jnp.exp2((old - top) * power)
                top_scr[i, g, :, t] = top
                top_scr[STEPS, g, :, t] = top
                total = jnp.zeros((8, TILE), jnp.float32)
                for k in range(0, CHUNK, SUB):
                    e = jnp.exp2((s_scr[n % 2, k : k + SUB, :] - top) * power)
                    total = total + jnp.sum(e.reshape(SUB // 8, 8, TILE), axis=0)
                    e_scr[g, i, k : k + SUB, t] = e.astype(jnp.bfloat16)
                total_scr[g, :, t] = total_scr[g, :, t] * fade + jnp.sum(total, axis=0, keepdims=True)
                att_acc[g, :, t] = att_acc[g, :, t] * fade + dot(v, e_scr[g, i, :, t], TN)

        @pl.loop(0, count)
        def _(i):
            inner = (i > 0) & (end - (i + 1) * CHUNK >= last_low)

            @pl.when(inner)
            def _():
                forward(i, True)

            @pl.when(jnp.logical_not(inner))
            def _():
                forward(i, False)

        inverse, delta = [], []
        for g in range(groups):
            inv = 1.0 / total_scr[g]
            att = (att_acc[g] * inv).astype(jnp.bfloat16)
            out_buf[slot, 0, :, g] = att.T.reshape(BLOCK, 8, width)
            do_t = do_scr[g].T.astype(jnp.float32)
            inverse.append(inv)
            delta.append(jnp.sum(att.astype(jnp.float32) * do_t, axis=0, keepdims=True))

        @pl.loop(0, count)
        def _(i):
            for g in range(groups):
                here = keys_at(i)
                p = e_scr[g, i].astype(jnp.float32) * (jnp.exp2((top_scr[i, g] - top_scr[STEPS, g]) * power) * inverse[g])
                dp = dp_scr[g, i]
                ds = (p * (dp - delta[g])).astype(jnp.bfloat16)
                dv_acc[g, here, :] += dot(p.astype(jnp.bfloat16), do_scr[g], NN)
                dk_acc[g, here, :] += dot(ds, q_scr[g], NN)
                dq_acc[g] += dot(k_win[g, here, :], ds, TN)

        for g in range(groups):
            out_buf[slot, 1, :, g] = (dq_acc[g] * scale).astype(jnp.bfloat16).T.reshape(BLOCK, 8, width)
        for which in range(2):

            @pl.when(slot == 0)
            def _():
                write(0, which).start()

            @pl.when(slot == 1)
            def _():
                write(1, which).start()

    for ref, index, at in pieces(*grad_bufs):
        for g in range(groups):
            ref[(*index, 0, g)] = (dk_acc[g, at, :] * scale).astype(ref.dtype)
            ref[(*index, 1, g)] = dv_acc[g, at, :].astype(ref.dtype)
    grad_writes = [
        pltpu.make_async_copy(buf, ref, grad_sem.at[i]) for i, (buf, ref) in enumerate(zip(grad_bufs, grad_refs))
    ]
    for copy in grad_writes:
        copy.start()
    for slot in range(2):
        for which in range(2):
            write(slot, which).wait()
    for copy in grad_writes:
        copy.wait()


def attend(start, last, lengths, q4, q_got, do4, do_got, keys, filled):
    groups = keys[0].shape[-3]
    rows = BLOCK * 8
    width = q4.shape[3]
    full = (BLOCK, groups, 8, width)
    away = pl.BlockSpec(memory_space=pl.ANY)
    block = (2, groups, BLOCK, width)
    shapes = [a.shape for a in keys]
    grads = [(2, *block)] * 2 + [(3, *block)] * 3 if last else [block, (4, 3, *block)]
    whole = jax.ShapeDtypeStruct(q4.shape, jnp.bfloat16)
    piece = jax.ShapeDtypeStruct(full, jnp.bfloat16)
    return pl.pallas_call(
        functools.partial(attend_kernel, start, len(keys), last),
        grid_spec=pltpu.PrefetchScalarGridSpec(
            num_scalar_prefetch=1,
            grid=(1,),
            in_specs=[away] * (4 + len(keys) + len(filled)),
            out_specs=[away] * (4 + len(grads)),
            scratch_shapes=[
                pltpu.VMEM((groups, WINDOW + BLOCK, width), jnp.bfloat16),
                pltpu.VMEM((groups, WINDOW + BLOCK, width), jnp.bfloat16),
                pltpu.VMEM((groups, STEPS, CHUNK, rows), jnp.bfloat16),
                pltpu.VMEM((2, CHUNK, TILE), jnp.float32),
                pltpu.VMEM((groups, STEPS, CHUNK, rows), jnp.float32),
                pltpu.VMEM((STEPS + 1, groups, 1, rows), jnp.float32),
                pltpu.VMEM((groups, 1, rows), jnp.float32),
                pltpu.VMEM((groups, width, rows), jnp.float32),
                pltpu.VMEM((groups, width, rows), jnp.float32),
                pltpu.VMEM((groups, WINDOW + BLOCK, width), jnp.float32),
                pltpu.VMEM((groups, WINDOW + BLOCK, width), jnp.float32),
                pltpu.VMEM((groups, rows, width), jnp.bfloat16),
                pltpu.VMEM((groups, rows, width), jnp.bfloat16),
                pltpu.VMEM((2, 2, *full), jnp.bfloat16),
                pltpu.VMEM((2, 2, *full), jnp.bfloat16),
            ]
            + [pltpu.VMEM(a, jnp.bfloat16) for a in shapes + grads]
            + [
                pltpu.SemaphoreType.DMA((2, 2)),
                pltpu.SemaphoreType.DMA((2, 2)),
                pltpu.SemaphoreType.DMA((6,)),
                pltpu.SemaphoreType.DMA((6,)),
            ],
        ),
        out_shape=[whole, piece, whole, piece]
        + [jax.ShapeDtypeStruct(a, jnp.bfloat16) for a in grads],
        input_output_aliases={5 + len(keys): 0, 6 + len(keys): 2} if filled else {},
        compiler_params=pltpu.CompilerParams(vmem_limit_bytes=56 * 1024 * 1024),
        cost_estimate=pl.CostEstimate(
            flops=COST * groups, bytes_accessed=6_000_000 * groups, transcendentals=2_000_000 * groups
        ),
        name="attend",
    )(lengths, q4, q_got, do4, do_got, *keys, *filled)


def shards(queries, key_states, value_states, grad_out, doc_lengths):
    tokens, heads, width = queries.shape
    kv_heads = key_states.shape[1]
    per = heads // kv_heads
    groups = kv_heads // 2
    lead = PARTS[0][1]
    ctx = lax.axis_index("ctx")
    x = lax.axis_index("tensor")
    core = ctx % 2

    swap = [(i, i ^ 1) for i in range(8)]
    up = [(i, i + 2) for i in range(6)]
    down = [(i + 2, i) for i in range(6)]
    ahead = {d: [(i, (i + d) % 4) for i in range(4)] for d in (1, 2, 3)}

    kv = jnp.stack([key_states, value_states]).transpose(0, 2, 1, 3).reshape(2, 2, groups, tokens, width)
    kv_own = lax.dynamic_index_in_dim(kv, core, 1, keepdims=False)
    kv_send = lax.dynamic_index_in_dim(kv, 1 - core, 1, keepdims=False)
    kv_got = lax.ppermute(kv_send, "ctx", swap)
    row = jnp.stack([jnp.where(core == 0, kv_own, kv_got), jnp.where(core == 0, kv_got, kv_own)])

    q4 = queries.reshape(tokens, kv_heads, per, width)
    do4 = grad_out.reshape(tokens, kv_heads, per, width)
    q_send = lax.dynamic_slice_in_dim(q4, groups * (1 - core), groups, 1)
    do_send = lax.dynamic_slice_in_dim(do4, groups * (1 - core), groups, 1)

    before = [lax.ppermute(row[:, :, :lead], "ctx", up)]
    q_got = lax.ppermute(q_send, "ctx", swap)
    do_got = lax.ppermute(do_send, "ctx", swap)
    trade = functools.partial(lax.all_to_all, axis_name="tensor", split_axis=0, concat_axis=0, tiled=True)
    earlier, others, firsts = [], [], []
    for start, size in PARTS:
        first, second = row[:, :, start : start + size]
        old = before[0] if start == 0 else before[1][:, :, start - lead : start - lead + size]
        one = [jnp.stack([old[1], jnp.where(d < x, old[0], second)]) for d in range(4)]
        if start == 0:
            firsts = [first] + [lax.ppermute(first, "tensor", ahead[d]) for d in (1, 2, 3)]
            one, firsts, rest = lax.optimization_barrier((jnp.stack(one), firsts, row[:, :, lead:]))
            before.append(lax.ppermute(rest, "ctx", up))
            others.append(trade(one))
        else:
            sends = [jnp.stack([old[1], jnp.where(x + d >= 4, old[0], second), first]) for d in (1, 2, 3)]
            others.append([old, row[:, :, start : start + size]])
            others[-1] += [lax.ppermute(m, "tensor", ahead[d]) for d, m in enumerate(sends, 1)]
        earlier.append(old[0])

    filled, sent = [], []
    for part, (start, _) in enumerate(PARTS):
        last = part == len(PARTS) - 1
        keys = others[part] if part else [earlier[0], others[0], *firsts]
        att, att_send, dq, dq_send, *grad = attend(
            start, last, doc_lengths, q4, q_got, do4, do_got, keys, filled
        )
        filled = [att, dq]
        sent.append([lax.ppermute(att_send, "ctx", swap), lax.ppermute(dq_send, "ctx", swap)])
        if last:
            sends, raw = lax.optimization_barrier((grad[2:], raw))
            back = [lax.ppermute(p, "tensor", ahead[4 - d]) for d, p in enumerate(sends, 1)]
            old, own, *back = [t.astype(jnp.float32) for t in (*grad[:2], *back)]
            tail = (
                own[0] + sum(b[2] for b in back),
                own[1] + sum(jnp.where(x + d >= 4, 0, b[1]) for d, b in enumerate(back, 1)),
                old[0] + sum(jnp.where(x + d >= 4, b[1], 0) for d, b in enumerate(back, 1)),
                old[1] + sum(b[0] for b in back),
            )
        else:
            early, raw = grad[0].astype(jnp.float32), trade(grad[1])

    raw, sent[-1] = lax.optimization_barrier((raw, sent[-1]))
    back = raw.astype(jnp.float32)
    second = jnp.zeros_like(early)
    for d in range(4):
        early = early + jnp.where(d < x, back[d, 1], 0)
        second = second + jnp.where(d < x, 0, back[d, 1])
    head = (jnp.sum(back[:, 2], axis=0), second, early, jnp.sum(back[:, 0], axis=0))
    sums = [(a, b, jnp.stack([c, d]).astype(jnp.bfloat16)) for a, b, c, d in (head, tail)]

    def settle(full, index):
        for (start, _), got in zip(PARTS, sent):
            full = lax.dynamic_update_slice_in_dim(full, got[index], groups * (1 - core) + start, 1)
        return full.reshape(tokens, heads, width)

    attended, grad_queries = settle(filled[0], 0), settle(filled[1], 1)

    def finish(first, second, send):
        got = lax.ppermute(send, "ctx", down).astype(jnp.float32)
        both = jnp.stack([first + got[0], second + got[1]]).astype(jnp.bfloat16)
        mine = lax.dynamic_index_in_dim(both, core, 0, keepdims=False)
        theirs = lax.ppermute(lax.dynamic_index_in_dim(both, 1 - core, 0, keepdims=False), "ctx", swap)
        return jnp.where(core == 0, mine, theirs), jnp.where(core == 0, theirs, mine)

    head = [jnp.concatenate(t, axis=-3) for t in zip(*sums[:-1])]
    first, second, send = sums[-1]
    send, attended, grad_queries = lax.optimization_barrier((send, attended, grad_queries))
    done, at = {}, 0
    whole = finish(*head)
    for start, size in PARTS[:-1]:
        done[start] = [h[:, at : at + size] for h in whole]
        at += size
    done[PARTS[-1][0]] = finish(first, second, send)
    kv_grad = jnp.concatenate([done[start][core_half] for core_half in range(2) for start in sorted(done)], axis=1)
    kv_grad = kv_grad.transpose(0, 2, 1, 3)
    return attended, grad_queries, kv_grad[0], kv_grad[1]


def solution(mesh):
    placed = P(("dp", "ctx", "tensor"), None, None)
    return jax.shard_map(
        shards,
        mesh=mesh,
        in_specs=(placed, placed, placed, placed, P("dp")),
        out_specs=(placed, placed, placed, placed),
        check_vma=False,
    )
```

```python
import functools

import jax
import jax.numpy as jnp
from jax import lax
from jax.experimental import pallas as pl
from jax.experimental.pallas import tpu as pltpu
from jax.sharding import PartitionSpec as P

BLOCK = 128
SUB = 32
TILE = 512
CHUNK = 256
PARTS = ((0, 2), (2, 2))
WINDOW = 2048
STEPS = 5
COST = 15_000_000_000
LOG2E = 1.4426950408889634
MASKED = -1e30

NT = (((1,), (1,)), ((), ()))
NN = (((1,), (0,)), ((), ()))
TN = (((0,), (0,)), ((), ()))


def dot(a, b, dims):
    return lax.dot_general(a, b, dims, preferred_element_type=jnp.float32)


def attend_kernel(start, keys, last, lengths, q4, q_got, do4, do_got, *refs):
    results = 5 if last else 2
    *refs, in_sem, out_sem, key_sem, grad_sem = refs
    key_refs = refs[:keys]
    refs, grad_bufs = refs[:-results], refs[-results:]
    refs, key_bufs = refs[:-keys], refs[-keys:]
    (
        k_win,
        v_win,
        e_scr,
        s_scr,
        dp_scr,
        top_scr,
        total_scr,
        att_acc,
        dq_acc,
        dk_acc,
        dv_acc,
        q_scr,
        do_scr,
        in_buf,
        out_buf,
    ) = refs[-15:]
    att_own, att_send, dq_own, dq_send, *grad_refs = refs[-15 - 4 - results : -15]
    x = lax.axis_index("tensor")
    ctx = lax.axis_index("ctx")
    y, core = ctx // 2, ctx % 2
    ends = [lengths[0]]
    for i in range(1, lengths.shape[0]):
        ends.append(ends[-1] + lengths[i])

    def document(pos):
        begin = jnp.zeros_like(pos)
        for last in ends:
            begin = jnp.where(last <= pos, last, begin)
        return begin

    groups, rows, width = q_scr.shape
    ours = pl.ds(q_got.shape[1] * core + start, groups)
    here_got = pl.ds(start, groups)

    def read(slot, which):
        source = ((q4, do4), (q_got, do_got))[slot][which].at[:, (ours, here_got)[slot]]
        return pltpu.make_async_copy(source, in_buf.at[slot, which], in_sem.at[slot, which])

    def write(slot, which):
        target = ((att_own, dq_own), (att_send, dq_send))[slot][which]
        target = target.at[:, ours] if slot == 0 else target
        return pltpu.make_async_copy(out_buf.at[slot, which], target, out_sem.at[slot, which])

    key_reads = [
        pltpu.make_async_copy(ref, buf, key_sem.at[i]) for i, (ref, buf) in enumerate(zip(key_refs, key_bufs))
    ]
    for copy in key_reads:
        copy.start()
    for slot in range(2):
        for which in range(2):
            read(slot, which).start()
    scale = width**-0.5
    power = scale * LOG2E

    def place(block):
        return pl.ds(pl.multiple_of((block + 1) * BLOCK, BLOCK), BLOCK)

    def pieces(*bufs):
        found = []
        if len(bufs) == 5:
            before, own, *around = bufs
            for half in range(2):
                found.append((own, (half,), 8 + 4 * half + x))
                found.append((before, (half,), 4 * half + x))
            for shift, ref in enumerate(around, 1):
                source = lax.rem(x + 4 - shift, 4)
                found.append((ref, (0,), 4 + source))
                found.append((ref, (1,), jnp.where(source > x, source, 12 + source)))
                found.append((ref, (2,), 8 + source))
            return [(ref, index, place(block)) for ref, index, block in found]
        early, others, *around = bufs
        for shift, ref in enumerate(around):
            found.append((ref, (), 8 + lax.rem(x + 4 - shift, 4)))
        if not around:
            found = [(others, (d, 2), 8 + d) for d in range(4)]
        found.append((early, (), x))
        for d in range(4):
            found.append((others, (d, 0), 4 + d))
            found.append((others, (d, 1), jnp.where(d > x, d, 12 + d)))
        return [(ref, index, place(block)) for ref, index, block in found]

    k_win[...] = jnp.zeros_like(k_win)
    v_win[...] = jnp.zeros_like(v_win)
    dk_acc[...] = jnp.zeros_like(dk_acc)
    dv_acc[...] = jnp.zeros_like(dv_acc)
    for copy in key_reads:
        copy.wait()
    for ref, index, at in pieces(*key_bufs):
        for g in range(groups):
            k_win[g, at, :] = ref[(*index, 0, g)]
            v_win[g, at, :] = ref[(*index, 1, g)]

    @pl.loop(0, 2)
    def _(slot):
        for which, scr in enumerate((q_scr, do_scr)):
            pltpu.make_async_copy(q_got.at[:, here_got], in_buf.at[slot, which], in_sem.at[slot, which]).wait()
            for g in range(groups):
                scr[g] = in_buf[slot, which, :, g].reshape(rows, width)
        base = (y - 1) * (WINDOW // 2)
        begin = (8 + 4 * jnp.where(slot == 0, core, 1 - core) + x) * BLOCK
        end = begin + BLOCK
        count = (end - 1 - (document(base + begin) - base)) // CHUNK + 1
        last_low = document(base + end - 1) - base
        token = begin + lax.broadcasted_iota(jnp.int32, (1, rows), 1) // (rows // BLOCK)
        low = document(base + token) - base
        span = token - low
        top_scr[STEPS] = jnp.full((groups, 1, rows), MASKED, jnp.float32)
        total_scr[...] = jnp.zeros_like(total_scr)
        att_acc[...] = jnp.zeros_like(att_acc)
        dq_acc[...] = jnp.zeros_like(dq_acc)

        def keys_at(i):
            return pl.ds(pl.multiple_of(end + BLOCK - (i + 1) * CHUNK, BLOCK), CHUNK)

        def forward(i, inner):
            here = keys_at(i)
            tiles = [(g, slice(t, t + TILE)) for g in range(groups) for t in range(0, rows, TILE)]
            offset = lax.broadcasted_iota(jnp.int32, (CHUNK, TILE), 0) + (end - (i + 1) * CHUNK)

            def score(n):
                g, t = tiles[n]
                s = dot(k_win[g, here, :], q_scr[g, t, :], NT)
                if not inner:
                    past = (offset - low[:, t]).astype(jnp.uint32)
                    s = jnp.where(past <= span[:, t].astype(jnp.uint32), s, MASKED)
                s_scr[n % 2] = s
                return jnp.max(s, axis=0, keepdims=True)

            ahead = score(0)
            for n, (g, t) in enumerate(tiles):
                high = ahead
                if n + 1 < len(tiles):
                    ahead = score(n + 1)
                v = v_win[g, here, :]
                dp_scr[g, i, :, t] = dot(v, do_scr[g, t, :], NT)
                old = top_scr[STEPS, g, :, t]
                top = jnp.maximum(old, high)
                fade = jnp.exp2((old - top) * power)
                top_scr[i, g, :, t] = top
                top_scr[STEPS, g, :, t] = top
                total = jnp.zeros((8, TILE), jnp.float32)
                for k in range(0, CHUNK, SUB):
                    e = jnp.exp2((s_scr[n % 2, k : k + SUB, :] - top) * power)
                    total = total + jnp.sum(e.reshape(SUB // 8, 8, TILE), axis=0)
                    e_scr[g, i, k : k + SUB, t] = e.astype(jnp.bfloat16)
                total_scr[g, :, t] = total_scr[g, :, t] * fade + jnp.sum(total, axis=0, keepdims=True)
                att_acc[g, :, t] = att_acc[g, :, t] * fade + dot(v, e_scr[g, i, :, t], TN)

        @pl.loop(0, count)
        def _(i):
            inner = (i > 0) & (end - (i + 1) * CHUNK >= last_low)

            @pl.when(inner)
            def _():
                forward(i, True)

            @pl.when(jnp.logical_not(inner))
            def _():
                forward(i, False)

        inverse, delta = [], []
        for g in range(groups):
            inv = 1.0 / total_scr[g]
            att = (att_acc[g] * inv).astype(jnp.bfloat16)
            out_buf[slot, 0, :, g] = att.T.reshape(BLOCK, 8, width)
            do_t = do_scr[g].T.astype(jnp.float32)
            inverse.append(inv)
            delta.append(jnp.sum(att.astype(jnp.float32) * do_t, axis=0, keepdims=True))

        @pl.loop(0, count)
        def _(i):
            for g in range(groups):
                here = keys_at(i)
                p = e_scr[g, i].astype(jnp.float32) * (jnp.exp2((top_scr[i, g] - top_scr[STEPS, g]) * power) * inverse[g])
                dp = dp_scr[g, i]
                ds = (p * (dp - delta[g])).astype(jnp.bfloat16)
                dv_acc[g, here, :] += dot(p.astype(jnp.bfloat16), do_scr[g], NN)
                dk_acc[g, here, :] += dot(ds, q_scr[g], NN)
                dq_acc[g] += dot(k_win[g, here, :], ds, TN)

        for g in range(groups):
            out_buf[slot, 1, :, g] = (dq_acc[g] * scale).astype(jnp.bfloat16).T.reshape(BLOCK, 8, width)
        for which in range(2):

            @pl.when(slot == 0)
            def _():
                write(0, which).start()

            @pl.when(slot == 1)
            def _():
                write(1, which).start()

    for ref, index, at in pieces(*grad_bufs):
        for g in range(groups):
            ref[(*index, 0, g)] = (dk_acc[g, at, :] * scale).astype(ref.dtype)
            ref[(*index, 1, g)] = dv_acc[g, at, :].astype(ref.dtype)
    grad_writes = [
        pltpu.make_async_copy(buf, ref, grad_sem.at[i]) for i, (buf, ref) in enumerate(zip(grad_bufs, grad_refs))
    ]
    for copy in grad_writes:
        copy.start()
    for slot in range(2):
        for which in range(2):
            write(slot, which).wait()
    for copy in grad_writes:
        copy.wait()


def attend(start, last, lengths, q4, q_got, do4, do_got, keys, filled):
    groups = keys[0].shape[-3]
    rows = BLOCK * 8
    width = q4.shape[3]
    full = (BLOCK, groups, 8, width)
    away = pl.BlockSpec(memory_space=pl.ANY)
    block = (2, groups, BLOCK, width)
    shapes = [a.shape for a in keys]
    grads = [(2, *block)] * 2 + [(3, *block)] * 3 if last else [block, (4, 3, *block)]
    whole = jax.ShapeDtypeStruct(q4.shape, jnp.bfloat16)
    piece = jax.ShapeDtypeStruct(full, jnp.bfloat16)
    return pl.pallas_call(
        functools.partial(attend_kernel, start, len(keys), last),
        grid_spec=pltpu.PrefetchScalarGridSpec(
            num_scalar_prefetch=1,
            grid=(1,),
            in_specs=[away] * (4 + len(keys) + len(filled)),
            out_specs=[away] * (4 + len(grads)),
            scratch_shapes=[
                pltpu.VMEM((groups, WINDOW + BLOCK, width), jnp.bfloat16),
                pltpu.VMEM((groups, WINDOW + BLOCK, width), jnp.bfloat16),
                pltpu.VMEM((groups, STEPS, CHUNK, rows), jnp.bfloat16),
                pltpu.VMEM((2, CHUNK, TILE), jnp.float32),
                pltpu.VMEM((groups, STEPS, CHUNK, rows), jnp.float32),
                pltpu.VMEM((STEPS + 1, groups, 1, rows), jnp.float32),
                pltpu.VMEM((groups, 1, rows), jnp.float32),
                pltpu.VMEM((groups, width, rows), jnp.float32),
                pltpu.VMEM((groups, width, rows), jnp.float32),
                pltpu.VMEM((groups, WINDOW + BLOCK, width), jnp.float32),
                pltpu.VMEM((groups, WINDOW + BLOCK, width), jnp.float32),
                pltpu.VMEM((groups, rows, width), jnp.bfloat16),
                pltpu.VMEM((groups, rows, width), jnp.bfloat16),
                pltpu.VMEM((2, 2, *full), jnp.bfloat16),
                pltpu.VMEM((2, 2, *full), jnp.bfloat16),
            ]
            + [pltpu.VMEM(a, jnp.bfloat16) for a in shapes + grads]
            + [
                pltpu.SemaphoreType.DMA((2, 2)),
                pltpu.SemaphoreType.DMA((2, 2)),
                pltpu.SemaphoreType.DMA((6,)),
                pltpu.SemaphoreType.DMA((6,)),
            ],
        ),
        out_shape=[whole, piece, whole, piece]
        + [jax.ShapeDtypeStruct(a, jnp.bfloat16) for a in grads],
        input_output_aliases={5 + len(keys): 0, 6 + len(keys): 2} if filled else {},
        compiler_params=pltpu.CompilerParams(vmem_limit_bytes=56 * 1024 * 1024),
        cost_estimate=pl.CostEstimate(
            flops=COST * groups, bytes_accessed=6_000_000 * groups, transcendentals=2_000_000 * groups
        ),
        name="attend",
    )(lengths, q4, q_got, do4, do_got, *keys, *filled)


def shards(queries, key_states, value_states, grad_out, doc_lengths):
    tokens, heads, width = queries.shape
    kv_heads = key_states.shape[1]
    per = heads // kv_heads
    groups = kv_heads // 2
    lead = PARTS[0][1]
    ctx = lax.axis_index("ctx")
    x = lax.axis_index("tensor")
    core = ctx % 2

    swap = [(i, i ^ 1) for i in range(8)]
    up = [(i, i + 2) for i in range(6)]
    down = [(i + 2, i) for i in range(6)]
    ahead = {d: [(i, (i + d) % 4) for i in range(4)] for d in (1, 2, 3)}

    kv = jnp.stack([key_states, value_states]).transpose(0, 2, 1, 3).reshape(2, 2, groups, tokens, width)
    kv_own = lax.dynamic_index_in_dim(kv, core, 1, keepdims=False)
    kv_send = lax.dynamic_index_in_dim(kv, 1 - core, 1, keepdims=False)
    kv_got = lax.ppermute(kv_send, "ctx", swap)
    row = jnp.stack([jnp.where(core == 0, kv_own, kv_got), jnp.where(core == 0, kv_got, kv_own)])

    q4 = queries.reshape(tokens, kv_heads, per, width)
    do4 = grad_out.reshape(tokens, kv_heads, per, width)
    q_send = lax.dynamic_slice_in_dim(q4, groups * (1 - core), groups, 1)
    do_send = lax.dynamic_slice_in_dim(do4, groups * (1 - core), groups, 1)

    before = [lax.ppermute(row[:, :, :lead], "ctx", up), lax.ppermute(row[:, :, lead:], "ctx", up)]
    q_got = lax.ppermute(q_send, "ctx", swap)
    do_got = lax.ppermute(do_send, "ctx", swap)
    trade = functools.partial(lax.all_to_all, axis_name="tensor", split_axis=0, concat_axis=0, tiled=True)
    earlier, others, firsts = [], [], []
    for start, size in PARTS:
        first, second = row[:, :, start : start + size]
        old = before[0] if start == 0 else before[1][:, :, start - lead : start - lead + size]
        one = [jnp.stack([old[1], jnp.where(d < x, old[0], second)]) for d in range(4)]
        if start == 0:
            firsts = [first] + [lax.ppermute(first, "tensor", ahead[d]) for d in (1, 2, 3)]
            one, firsts = lax.optimization_barrier((jnp.stack(one), firsts))
            others.append(trade(one))
        else:
            sends = [jnp.stack([old[1], jnp.where(x + d >= 4, old[0], second), first]) for d in (1, 2, 3)]
            others.append([old, row[:, :, start : start + size]])
            others[-1] += [lax.ppermute(m, "tensor", ahead[d]) for d, m in enumerate(sends, 1)]
        earlier.append(old[0])

    filled, sent = [], []
    for part, (start, _) in enumerate(PARTS):
        last = part == len(PARTS) - 1
        keys = others[part] if part else [earlier[0], others[0], *firsts]
        att, att_send, dq, dq_send, *grad = attend(
            start, last, doc_lengths, q4, q_got, do4, do_got, keys, filled
        )
        filled = [att, dq]
        sent.append([lax.ppermute(att_send, "ctx", swap), lax.ppermute(dq_send, "ctx", swap)])
        if last:
            sends, raw = lax.optimization_barrier((grad[2:], raw))
            back = [lax.ppermute(p, "tensor", ahead[4 - d]) for d, p in enumerate(sends, 1)]
            old, own, *back = [t.astype(jnp.float32) for t in (*grad[:2], *back)]
            tail = (
                own[0] + sum(b[2] for b in back),
                own[1] + sum(jnp.where(x + d >= 4, 0, b[1]) for d, b in enumerate(back, 1)),
                old[0] + sum(jnp.where(x + d >= 4, b[1], 0) for d, b in enumerate(back, 1)),
                old[1] + sum(b[0] for b in back),
            )
        else:
            early, raw = grad[0].astype(jnp.float32), trade(grad[1])

    raw, sent[-1] = lax.optimization_barrier((raw, sent[-1]))
    back = raw.astype(jnp.float32)
    second = jnp.zeros_like(early)
    for d in range(4):
        early = early + jnp.where(d < x, back[d, 1], 0)
        second = second + jnp.where(d < x, 0, back[d, 1])
    head = (jnp.sum(back[:, 2], axis=0), second, early, jnp.sum(back[:, 0], axis=0))
    sums = [(a, b, jnp.stack([c, d]).astype(jnp.bfloat16)) for a, b, c, d in (head, tail)]

    def settle(full, index):
        for (start, _), got in zip(PARTS, sent):
            full = lax.dynamic_update_slice_in_dim(full, got[index], groups * (1 - core) + start, 1)
        return full.reshape(tokens, heads, width)

    attended, grad_queries = settle(filled[0], 0), settle(filled[1], 1)

    def finish(first, second, send):
        got = lax.ppermute(send, "ctx", down).astype(jnp.float32)
        both = jnp.stack([first + got[0], second + got[1]]).astype(jnp.bfloat16)
        mine = lax.dynamic_index_in_dim(both, core, 0, keepdims=False)
        theirs = lax.ppermute(lax.dynamic_index_in_dim(both, 1 - core, 0, keepdims=False), "ctx", swap)
        return jnp.where(core == 0, mine, theirs), jnp.where(core == 0, theirs, mine)

    head = [jnp.concatenate(t, axis=-3) for t in zip(*sums[:-1])]
    first, second, send = sums[-1]
    send, attended, grad_queries = lax.optimization_barrier((send, attended, grad_queries))
    done, at = {}, 0
    whole = finish(*head)
    for start, size in PARTS[:-1]:
        done[start] = [h[:, at : at + size] for h in whole]
        at += size
    done[PARTS[-1][0]] = finish(first, second, send)
    kv_grad = jnp.concatenate([done[start][core_half] for core_half in range(2) for start in sorted(done)], axis=1)
    kv_grad = kv_grad.transpose(0, 2, 1, 3)
    return attended, grad_queries, kv_grad[0], kv_grad[1]


def solution(mesh):
    placed = P(("dp", "ctx", "tensor"), None, None)
    return jax.shard_map(
        shards,
        mesh=mesh,
        in_specs=(placed, placed, placed, placed, P("dp")),
        out_specs=(placed, placed, placed, placed),
        check_vma=False,
    )
```

```python
import functools

import jax
import jax.numpy as jnp
from jax import lax
from jax.experimental import pallas as pl
from jax.experimental.pallas import tpu as pltpu
from jax.sharding import PartitionSpec as P

BLOCK = 128
SUB = 32
TILE = 512
CHUNK = 256
PARTS = ((0, 2), (2, 2))
WINDOW = 2048
STEPS = 5
COST = 15_000_000_000
LOG2E = 1.4426950408889634
MASKED = -1e30

NT = (((1,), (1,)), ((), ()))
NN = (((1,), (0,)), ((), ()))
TN = (((0,), (0,)), ((), ()))


def dot(a, b, dims):
    return lax.dot_general(a, b, dims, preferred_element_type=jnp.float32)


def attend_kernel(start, keys, last, lengths, q4, q_got, do4, do_got, *refs):
    results = 5 if last else 2
    *refs, in_sem, out_sem, key_sem, grad_sem = refs
    key_refs = refs[:keys]
    refs, grad_bufs = refs[:-results], refs[-results:]
    refs, key_bufs = refs[:-keys], refs[-keys:]
    (
        k_win,
        v_win,
        e_scr,
        s_scr,
        dp_scr,
        top_scr,
        total_scr,
        att_acc,
        dq_acc,
        dk_acc,
        dv_acc,
        q_scr,
        do_scr,
        in_buf,
        out_buf,
    ) = refs[-15:]
    att_own, att_send, dq_own, dq_send, *grad_refs = refs[-15 - 4 - results : -15]
    x = lax.axis_index("tensor")
    ctx = lax.axis_index("ctx")
    y, core = ctx // 2, ctx % 2
    ends = [lengths[0]]
    for i in range(1, lengths.shape[0]):
        ends.append(ends[-1] + lengths[i])

    def document(pos):
        begin = jnp.zeros_like(pos)
        for last in ends:
            begin = jnp.where(last <= pos, last, begin)
        return begin

    groups, rows, width = q_scr.shape
    ours = pl.ds(q_got.shape[1] * core + start, groups)
    here_got = pl.ds(start, groups)

    def read(slot, which):
        source = ((q4, do4), (q_got, do_got))[slot][which].at[:, (ours, here_got)[slot]]
        return pltpu.make_async_copy(source, in_buf.at[slot, which], in_sem.at[slot, which])

    def write(slot, which):
        target = ((att_own, dq_own), (att_send, dq_send))[slot][which]
        target = target.at[:, ours] if slot == 0 else target
        return pltpu.make_async_copy(out_buf.at[slot, which], target, out_sem.at[slot, which])

    key_reads = [
        pltpu.make_async_copy(ref, buf, key_sem.at[i]) for i, (ref, buf) in enumerate(zip(key_refs, key_bufs))
    ]
    for copy in key_reads:
        copy.start()
    for slot in range(2):
        for which in range(2):
            read(slot, which).start()
    scale = width**-0.5
    power = scale * LOG2E

    def place(block):
        return pl.ds(pl.multiple_of((block + 1) * BLOCK, BLOCK), BLOCK)

    def pieces(*bufs):
        found = []
        if len(bufs) == 5:
            before, own, *around = bufs
            for half in range(2):
                found.append((own, (half,), 8 + 4 * half + x))
                found.append((before, (half,), 4 * half + x))
            for shift, ref in enumerate(around, 1):
                source = lax.rem(x + 4 - shift, 4)
                found.append((ref, (0,), 4 + source))
                found.append((ref, (1,), jnp.where(source > x, source, 12 + source)))
                found.append((ref, (2,), 8 + source))
            return [(ref, index, place(block)) for ref, index, block in found]
        early, others, *around = bufs
        for shift, ref in enumerate(around):
            found.append((ref, (), 8 + lax.rem(x + 4 - shift, 4)))
        if not around:
            found = [(others, (d, 2), 8 + d) for d in range(4)]
        found.append((early, (), x))
        for d in range(4):
            found.append((others, (d, 0), 4 + d))
            found.append((others, (d, 1), jnp.where(d > x, d, 12 + d)))
        return [(ref, index, place(block)) for ref, index, block in found]

    k_win[...] = jnp.zeros_like(k_win)
    v_win[...] = jnp.zeros_like(v_win)
    dk_acc[...] = jnp.zeros_like(dk_acc)
    dv_acc[...] = jnp.zeros_like(dv_acc)
    for copy in key_reads:
        copy.wait()
    for ref, index, at in pieces(*key_bufs):
        for g in range(groups):
            k_win[g, at, :] = ref[(*index, 0, g)]
            v_win[g, at, :] = ref[(*index, 1, g)]

    @pl.loop(0, 2)
    def _(slot):
        for which, scr in enumerate((q_scr, do_scr)):
            pltpu.make_async_copy(q_got.at[:, here_got], in_buf.at[slot, which], in_sem.at[slot, which]).wait()
            for g in range(groups):
                scr[g] = in_buf[slot, which, :, g].reshape(rows, width)
        base = (y - 1) * (WINDOW // 2)
        begin = (8 + 4 * jnp.where(slot == 0, core, 1 - core) + x) * BLOCK
        end = begin + BLOCK
        count = (end - 1 - (document(base + begin) - base)) // CHUNK + 1
        last_low = document(base + end - 1) - base
        token = begin + lax.broadcasted_iota(jnp.int32, (1, rows), 1) // (rows // BLOCK)
        low = document(base + token) - base
        span = token - low
        top_scr[STEPS] = jnp.full((groups, 1, rows), MASKED, jnp.float32)
        total_scr[...] = jnp.zeros_like(total_scr)
        att_acc[...] = jnp.zeros_like(att_acc)
        dq_acc[...] = jnp.zeros_like(dq_acc)

        def keys_at(i):
            return pl.ds(pl.multiple_of(end + BLOCK - (i + 1) * CHUNK, BLOCK), CHUNK)

        def forward(i, inner):
            here = keys_at(i)
            tiles = [(g, slice(t, t + TILE)) for g in range(groups) for t in range(0, rows, TILE)]
            offset = lax.broadcasted_iota(jnp.int32, (CHUNK, TILE), 0) + (end - (i + 1) * CHUNK)

            def score(n):
                g, t = tiles[n]
                s = dot(k_win[g, here, :], q_scr[g, t, :], NT)
                if not inner:
                    past = (offset - low[:, t]).astype(jnp.uint32)
                    s = jnp.where(past <= span[:, t].astype(jnp.uint32), s, MASKED)
                s_scr[n % 2] = s
                return jnp.max(s, axis=0, keepdims=True)

            ahead = score(0)
            for n, (g, t) in enumerate(tiles):
                high = ahead
                if n + 1 < len(tiles):
                    ahead = score(n + 1)
                v = v_win[g, here, :]
                dp_scr[g, i, :, t] = dot(v, do_scr[g, t, :], NT)
                old = top_scr[STEPS, g, :, t]
                top = jnp.maximum(old, high)
                fade = jnp.exp2((old - top) * power)
                top_scr[i, g, :, t] = top
                top_scr[STEPS, g, :, t] = top
                total = jnp.zeros((8, TILE), jnp.float32)
                for k in range(0, CHUNK, SUB):
                    e = jnp.exp2((s_scr[n % 2, k : k + SUB, :] - top) * power)
                    total = total + jnp.sum(e.reshape(SUB // 8, 8, TILE), axis=0)
                    e_scr[g, i, k : k + SUB, t] = e.astype(jnp.bfloat16)
                total_scr[g, :, t] = total_scr[g, :, t] * fade + jnp.sum(total, axis=0, keepdims=True)
                att_acc[g, :, t] = att_acc[g, :, t] * fade + dot(v, e_scr[g, i, :, t], TN)

        @pl.loop(0, count)
        def _(i):
            inner = (i > 0) & (end - (i + 1) * CHUNK >= last_low)

            @pl.when(inner)
            def _():
                forward(i, True)

            @pl.when(jnp.logical_not(inner))
            def _():
                forward(i, False)

        inverse, delta = [], []
        for g in range(groups):
            inv = 1.0 / total_scr[g]
            att = (att_acc[g] * inv).astype(jnp.bfloat16)
            out_buf[slot, 0, :, g] = att.T.reshape(BLOCK, 8, width)
            do_t = do_scr[g].T.astype(jnp.float32)
            inverse.append(inv)
            delta.append(jnp.sum(att.astype(jnp.float32) * do_t, axis=0, keepdims=True))

        @pl.loop(0, count)
        def _(i):
            for g in range(groups):
                here = keys_at(i)
                p = e_scr[g, i].astype(jnp.float32) * (jnp.exp2((top_scr[i, g] - top_scr[STEPS, g]) * power) * inverse[g])
                dp = dp_scr[g, i]
                ds = (p * (dp - delta[g])).astype(jnp.bfloat16)
                dv_acc[g, here, :] += dot(p.astype(jnp.bfloat16), do_scr[g], NN)
                dk_acc[g, here, :] += dot(ds, q_scr[g], NN)
                dq_acc[g] += dot(k_win[g, here, :], ds, TN)

        for g in range(groups):
            out_buf[slot, 1, :, g] = (dq_acc[g] * scale).astype(jnp.bfloat16).T.reshape(BLOCK, 8, width)
        for which in range(2):

            @pl.when(slot == 0)
            def _():
                write(0, which).start()

            @pl.when(slot == 1)
            def _():
                write(1, which).start()

    for ref, index, at in pieces(*grad_bufs):
        for g in range(groups):
            ref[(*index, 0, g)] = (dk_acc[g, at, :] * scale).astype(ref.dtype)
            ref[(*index, 1, g)] = dv_acc[g, at, :].astype(ref.dtype)
    grad_writes = [
        pltpu.make_async_copy(buf, ref, grad_sem.at[i]) for i, (buf, ref) in enumerate(zip(grad_bufs, grad_refs))
    ]
    for copy in grad_writes:
        copy.start()
    for slot in range(2):
        for which in range(2):
            write(slot, which).wait()
    for copy in grad_writes:
        copy.wait()


def attend(start, last, lengths, q4, q_got, do4, do_got, keys, filled):
    groups = keys[0].shape[-3]
    rows = BLOCK * 8
    width = q4.shape[3]
    full = (BLOCK, groups, 8, width)
    away = pl.BlockSpec(memory_space=pl.ANY)
    block = (2, groups, BLOCK, width)
    shapes = [a.shape for a in keys]
    grads = [(2, *block)] * 2 + [(3, *block)] * 3 if last else [block, (4, 3, *block)]
    whole = jax.ShapeDtypeStruct(q4.shape, jnp.bfloat16)
    piece = jax.ShapeDtypeStruct(full, jnp.bfloat16)
    return pl.pallas_call(
        functools.partial(attend_kernel, start, len(keys), last),
        grid_spec=pltpu.PrefetchScalarGridSpec(
            num_scalar_prefetch=1,
            grid=(1,),
            in_specs=[away] * (4 + len(keys) + len(filled)),
            out_specs=[away] * (4 + len(grads)),
            scratch_shapes=[
                pltpu.VMEM((groups, WINDOW + BLOCK, width), jnp.bfloat16),
                pltpu.VMEM((groups, WINDOW + BLOCK, width), jnp.bfloat16),
                pltpu.VMEM((groups, STEPS, CHUNK, rows), jnp.bfloat16),
                pltpu.VMEM((2, CHUNK, TILE), jnp.float32),
                pltpu.VMEM((groups, STEPS, CHUNK, rows), jnp.float32),
                pltpu.VMEM((STEPS + 1, groups, 1, rows), jnp.float32),
                pltpu.VMEM((groups, 1, rows), jnp.float32),
                pltpu.VMEM((groups, width, rows), jnp.float32),
                pltpu.VMEM((groups, width, rows), jnp.float32),
                pltpu.VMEM((groups, WINDOW + BLOCK, width), jnp.float32),
                pltpu.VMEM((groups, WINDOW + BLOCK, width), jnp.float32),
                pltpu.VMEM((groups, rows, width), jnp.bfloat16),
                pltpu.VMEM((groups, rows, width), jnp.bfloat16),
                pltpu.VMEM((2, 2, *full), jnp.bfloat16),
                pltpu.VMEM((2, 2, *full), jnp.bfloat16),
            ]
            + [pltpu.VMEM(a, jnp.bfloat16) for a in shapes + grads]
            + [
                pltpu.SemaphoreType.DMA((2, 2)),
                pltpu.SemaphoreType.DMA((2, 2)),
                pltpu.SemaphoreType.DMA((6,)),
                pltpu.SemaphoreType.DMA((6,)),
            ],
        ),
        out_shape=[whole, piece, whole, piece]
        + [jax.ShapeDtypeStruct(a, jnp.bfloat16) for a in grads],
        input_output_aliases={5 + len(keys): 0, 6 + len(keys): 2} if filled else {},
        compiler_params=pltpu.CompilerParams(vmem_limit_bytes=56 * 1024 * 1024),
        cost_estimate=pl.CostEstimate(
            flops=COST * groups, bytes_accessed=6_000_000 * groups, transcendentals=2_000_000 * groups
        ),
        name="attend",
    )(lengths, q4, q_got, do4, do_got, *keys, *filled)


def shards(queries, key_states, value_states, grad_out, doc_lengths):
    tokens, heads, width = queries.shape
    kv_heads = key_states.shape[1]
    per = heads // kv_heads
    groups = kv_heads // 2
    lead = PARTS[0][1]
    ctx = lax.axis_index("ctx")
    x = lax.axis_index("tensor")
    core = ctx % 2

    swap = [(i, i ^ 1) for i in range(8)]
    up = [(i, i + 2) for i in range(6)]
    down = [(i + 2, i) for i in range(6)]
    ahead = {d: [(i, (i + d) % 4) for i in range(4)] for d in (1, 2, 3)}

    kv = jnp.stack([key_states, value_states]).transpose(0, 2, 1, 3).reshape(2, 2, groups, tokens, width)
    kv_own = lax.dynamic_index_in_dim(kv, core, 1, keepdims=False)
    kv_send = lax.dynamic_index_in_dim(kv, 1 - core, 1, keepdims=False)
    kv_got = lax.ppermute(kv_send, "ctx", swap)
    row = jnp.stack([jnp.where(core == 0, kv_own, kv_got), jnp.where(core == 0, kv_got, kv_own)])

    q4 = queries.reshape(tokens, kv_heads, per, width)
    do4 = grad_out.reshape(tokens, kv_heads, per, width)
    q_send = lax.dynamic_slice_in_dim(q4, groups * (1 - core), groups, 1)
    do_send = lax.dynamic_slice_in_dim(do4, groups * (1 - core), groups, 1)

    before = [lax.ppermute(row[:, :, :lead], "ctx", up)]
    q_got = lax.ppermute(q_send, "ctx", swap)
    do_got = lax.ppermute(do_send, "ctx", swap)
    trade = functools.partial(lax.all_to_all, axis_name="tensor", split_axis=0, concat_axis=0, tiled=True)
    earlier, others, firsts = [], [], []
    for start, size in PARTS:
        first, second = row[:, :, start : start + size]
        old = before[0] if start == 0 else before[1][:, :, start - lead : start - lead + size]
        one = [jnp.stack([old[1], jnp.where(d < x, old[0], second)]) for d in range(4)]
        if start == 0:
            firsts = [first] + [lax.ppermute(first, "tensor", ahead[d]) for d in (1, 2, 3)]
            one, firsts, rest = lax.optimization_barrier((jnp.stack(one), firsts, row[:, :, lead:]))
            before.append(lax.ppermute(rest, "ctx", up))
            others.append(trade(one))
        else:
            sends = [jnp.stack([old[1], jnp.where(x + d >= 4, old[0], second), first]) for d in (1, 2, 3)]
            others.append([old, row[:, :, start : start + size]])
            others[-1] += [lax.ppermute(m, "tensor", ahead[d]) for d, m in enumerate(sends, 1)]
        earlier.append(old[0])

    filled, sent = [], []
    for part, (start, _) in enumerate(PARTS):
        last = part == len(PARTS) - 1
        keys = others[part] if part else [earlier[0], others[0], *firsts]
        att, att_send, dq, dq_send, *grad = attend(
            start, last, doc_lengths, q4, q_got, do4, do_got, keys, filled
        )
        filled = [att, dq]
        sent.append([lax.ppermute(att_send, "ctx", swap), lax.ppermute(dq_send, "ctx", swap)])
        if last:
            sends, raw = lax.optimization_barrier((grad[2:], raw))
            back = [lax.ppermute(p, "tensor", ahead[4 - d]) for d, p in enumerate(sends, 1)]
            old, own, *back = [t.astype(jnp.float32) for t in (*grad[:2], *back)]
            tail = (
                own[0] + sum(b[2] for b in back),
                own[1] + sum(jnp.where(x + d >= 4, 0, b[1]) for d, b in enumerate(back, 1)),
                old[0] + sum(jnp.where(x + d >= 4, b[1], 0) for d, b in enumerate(back, 1)),
                old[1] + sum(b[0] for b in back),
            )
        else:
            early, raw = grad[0].astype(jnp.float32), trade(grad[1])

    def settle(full, index):
        for (start, _), got in zip(PARTS, sent):
            full = lax.dynamic_update_slice_in_dim(full, got[index], groups * (1 - core) + start, 1)
        return full.reshape(tokens, heads, width)

    attended, grad_queries = settle(filled[0], 0), settle(filled[1], 1)

    raw, attended = lax.optimization_barrier((raw, attended))
    back = raw.astype(jnp.float32)
    second = jnp.zeros_like(early)
    for d in range(4):
        early = early + jnp.where(d < x, back[d, 1], 0)
        second = second + jnp.where(d < x, 0, back[d, 1])
    head = (jnp.sum(back[:, 2], axis=0), second, early, jnp.sum(back[:, 0], axis=0))
    sums = [(a, b, jnp.stack([c, d]).astype(jnp.bfloat16)) for a, b, c, d in (head, tail)]

    def finish(first, second, send):
        got = lax.ppermute(send, "ctx", down).astype(jnp.float32)
        both = jnp.stack([first + got[0], second + got[1]]).astype(jnp.bfloat16)
        mine = lax.dynamic_index_in_dim(both, core, 0, keepdims=False)
        theirs = lax.ppermute(lax.dynamic_index_in_dim(both, 1 - core, 0, keepdims=False), "ctx", swap)
        return jnp.where(core == 0, mine, theirs), jnp.where(core == 0, theirs, mine)

    head = [jnp.concatenate(t, axis=-3) for t in zip(*sums[:-1])]
    first, second, send = sums[-1]
    send, attended, grad_queries = lax.optimization_barrier((send, attended, grad_queries))
    done, at = {}, 0
    whole = finish(*head)
    for start, size in PARTS[:-1]:
        done[start] = [h[:, at : at + size] for h in whole]
        at += size
    done[PARTS[-1][0]] = finish(first, second, send)
    kv_grad = jnp.concatenate([done[start][core_half] for core_half in range(2) for start in sorted(done)], axis=1)
    kv_grad = kv_grad.transpose(0, 2, 1, 3)
    return attended, grad_queries, kv_grad[0], kv_grad[1]


def solution(mesh):
    placed = P(("dp", "ctx", "tensor"), None, None)
    return jax.shard_map(
        shards,
        mesh=mesh,
        in_specs=(placed, placed, placed, placed, P("dp")),
        out_specs=(placed, placed, placed, placed),
        check_vma=False,
    )
```
